512 devices in a mesh: ctx: 32 (over x_hi, y, core), head: 16 (over x_lo, z).
Axes of the slice: x: 4 (x_hi: 2, x_lo: 2; x = x_hi * 2 + x_lo), y: 8, z: 8, core: 2. Of those that a mesh axis runs over, the one named last changes fastest.
Arguments:
- query: bfloat16 [4096, 4096], P('ctx', 'head'), may hold values from -5 to 5
- key: bfloat16 [4096, 4096], P('ctx', 'head'), may hold values from -5 to 5
- value: bfloat16 [4096, 4096], P('ctx', 'head'), may hold values from -6 to 6
- query_tangent: bfloat16 [4096, 4096], P('ctx', 'head'), may hold values from -6 to 6
- key_tangent: bfloat16 [4096, 4096], P('ctx', 'head'), may hold values from -6 to 6
- value_tangent: bfloat16 [4096, 4096], P('ctx', 'head'), may hold values from -6 to 6
- out_weight: bfloat16 [4096, 4096], P('head'), may hold values from -0.09375 to 0.09375
- block_mask: int32 [32, 32], replicated, may hold values from 0 to 1, as said below
- probe: int32 [4096, 4096], P(('ctx', 'head')), may hold values 0 or 1
Outputs:
- output: bfloat16 [4096, 4096], P(('ctx', 'head'))
- output_tangent: bfloat16 [4096, 4096], P(('ctx', 'head'))
- trace_terms: float32 [4096], P(('ctx', 'head'))
The draws below stay inside these ranges and needn't reach their ends.
Inputs may be any that keep to these rules, and one draw needn't show every extreme that they name: `block_mask`: entry (b, b) is 1 for every block b.
All inputs are finite; a program needn't handle non-finite values. No bound on the sum of `probe` on one device may be relied on, other than what follows from the above.
Results may differ from the reference program's by a relative error of at most 0.005.
Values may be sent and summed in bfloat16 or wider, within the bound.
A program may use at most 64 MiB of HBM per device.

```python
import math
import jax
import jax.numpy as jnp
from jax import lax

D = 4096
HEADS = 32
HD = 128
BLOCK = 128
TOKENS = 4096
NB = 32


def draw_query(key, part):
    base = jnp.clip(jax.random.normal(jax.random.fold_in(key, 1), (TOKENS, HEADS * HD), jnp.float32), -5.0, 5.0)
    return base.astype(jnp.bfloat16)


def draw_key(key, part):
    base = jnp.clip(jax.random.normal(jax.random.fold_in(key, 2), (TOKENS, HEADS * HD), jnp.float32), -5.0, 5.0)
    return base.astype(jnp.bfloat16)


def draw_block_mask(key, part):
    rates = jax.random.randint(jax.random.fold_in(key, 3), (NB, 1), 0, 5)
    rolls = jax.random.randint(jax.random.fold_in(key, 4), (NB, NB), 0, 20)
    diagonal = jnp.arange(NB)[:, None] == jnp.arange(NB)[None, :]
    return jnp.where((rolls < rates) | diagonal, 1, 0).astype(jnp.int32)


def set_ends(values, key, smallest, largest):
    place = [jax.random.randint(jax.random.fold_in(key, axis), (), 0, length) for axis, length in enumerate(values.shape)]
    widest = values.shape.index(max(values.shape))
    neighbour = place[:widest] + [(place[widest] + 1) % values.shape[widest]] + place[widest + 1:]
    return values.at[tuple(place)].set(smallest).at[tuple(neighbour)].set(largest)


def level_of(own_key, shape, cuts, low, high):
    gain, own = 1.0, jax.random.fold_in(own_key, 6)
    for position, shards_of in cuts:
        draws = jnp.exp(jax.random.uniform(jax.random.fold_in(own, position), (shards_of,), jnp.float32, low / len(cuts), high / len(cuts)))
        gain = gain * jnp.repeat(draws, shape[position] // shards_of).reshape([-1 if axis == position else 1 for axis in range(len(shape))])
    return gain


def bell_draw(own_key, shape, width, limit, split=(), held_as=jnp.bfloat16):
    values = jax.random.normal(own_key, shape, jnp.float32) * width
    if len(split) > 0:
        values = level_of(own_key, shape, split, -0.22, 0.18) * values
    return jnp.clip(values, min=-limit, max=limit).astype(held_as)


def setup_inputs(seed: int = 0) -> dict:
    splits = jax.random.split(jax.random.key(seed), 10)
    query = draw_query(jax.random.fold_in(splits[9], 71), 0)
    key = draw_key(jax.random.fold_in(splits[9], 71), 0)
    value = bell_draw(splits[2], (TOKENS, HEADS * HD), 1.0, 6.0, ((0, 32), (1, 16)))
    query_tangent = bell_draw(splits[3], (TOKENS, HEADS * HD), 1.0, 6.0, ((0, 32), (1, 16)))
    key_tangent = bell_draw(splits[4], (TOKENS, HEADS * HD), 1.0, 6.0, ((0, 32), (1, 16)))
    value_tangent = bell_draw(splits[5], (TOKENS, HEADS * HD), 1.0, 6.0, ((0, 32), (1, 16)))
    out_weight = bell_draw(splits[6], (HEADS * HD, D), (HEADS * HD) ** -0.5, 0.09375, ((0, 16),))
    block_mask = draw_block_mask(jax.random.fold_in(splits[9], 71), 0)
    probe = set_ends((jax.random.randint(splits[8], (TOKENS, D), 0, 2) < 1).astype(jnp.int32), jax.random.fold_in(splits[8], 1), 0, 1)
    return {"query": query, "key": key, "value": value, "query_tangent": query_tangent, "key_tangent": key_tangent, "value_tangent": value_tangent, "out_weight": out_weight, "block_mask": block_mask, "probe": probe}


def reference(query, key, value, query_tangent, key_tangent, value_tangent, out_weight, block_mask, probe):
    score_scale = 1.0 / math.sqrt(HD)
    key_full = key.astype(jnp.float32).reshape(TOKENS, HEADS, HD)
    key_dot = key_tangent.astype(jnp.float32).reshape(TOKENS, HEADS, HD)
    value_full = value.astype(jnp.float32).reshape(TOKENS, HEADS, HD)
    value_dot = value_tangent.astype(jnp.float32).reshape(TOKENS, HEADS, HD)
    highest = lax.Precision.HIGHEST

    def one_block(inputs):
        block_index, mask_row = inputs
        first_row = (block_index * BLOCK).astype(jnp.int32)
        query_rows = lax.dynamic_slice_in_dim(query, first_row, BLOCK, 0).astype(jnp.float32).reshape(BLOCK, HEADS, HD)
        query_dot = lax.dynamic_slice_in_dim(query_tangent, first_row, BLOCK, 0).astype(jnp.float32).reshape(BLOCK, HEADS, HD)
        allowed = jnp.repeat(mask_row, BLOCK) > 0
        scores = jnp.einsum('qhd,khd->hqk', query_rows, key_full, precision=highest) * score_scale
        slopes = (jnp.einsum('qhd,khd->hqk', query_dot, key_full, precision=highest) + jnp.einsum('qhd,khd->hqk', query_rows, key_dot, precision=highest)) * score_scale
        allowed_h = allowed[None, None, :]
        top_score = lax.optimization_barrier(jnp.max(jnp.where(allowed_h, scores, -1e+30), axis=-1))
        weights = jnp.where(allowed_h, jnp.exp(scores - top_score[..., None]), 0.0)
        tilted = weights * slopes
        total = lax.optimization_barrier(jnp.sum(weights, axis=-1))
        bend = lax.optimization_barrier(jnp.sum(tilted, axis=-1))
        mixed = jnp.einsum('hqk,khd->qhd', weights, value_full, precision=highest)
        mixed_dot = jnp.einsum('hqk,khd->qhd', weights, value_dot, precision=highest) + jnp.einsum('hqk,khd->qhd', tilted, value_full, precision=highest)
        total_q = total.T[:, :, None]
        attended = mixed / total_q
        attended_dot = mixed_dot / total_q - bend.T[:, :, None] / total_q * attended
        return (attended.reshape(BLOCK, HEADS * HD).astype(jnp.bfloat16), attended_dot.reshape(BLOCK, HEADS * HD).astype(jnp.bfloat16))
    attended, attended_dot = lax.map(one_block, (jnp.arange(NB, dtype=jnp.int32), block_mask))
    attended = attended.reshape(TOKENS, HEADS * HD)
    attended_dot = attended_dot.reshape(TOKENS, HEADS * HD)
    projected = jnp.dot(attended, out_weight, preferred_element_type=jnp.float32)
    projected_dot = jnp.dot(attended_dot, out_weight, preferred_element_type=jnp.float32)
    probe_sign = (2 * probe - 1).astype(jnp.float32)
    trace_terms = lax.optimization_barrier(jnp.sum(probe_sign * projected_dot, axis=1)) / math.sqrt(D)
    return (projected.astype(jnp.bfloat16), projected_dot.astype(jnp.bfloat16), trace_terms)
```

```python
import functools
import math

import jax
import jax.numpy as jnp
from jax import lax
from jax.experimental import pallas as pl
from jax.experimental.pallas import tpu as pltpu
from jax.sharding import PartitionSpec as P

HD = 128
BLOCK = 128
RING = 8
PAIR = 2 * BLOCK
MASKED = -1e30
FLOWS = 4
SCALE = 1.0 / math.sqrt(HD)
SCALE2 = SCALE * math.log2(math.e)


def dot(a, b):
    return jnp.dot(a, b, preferred_element_type=jnp.float32)


def dot_t(a, b):
    return lax.dot_general(a, b, (((1,), (1,)), ((), ())), preferred_element_type=jnp.float32)


def kernel(
    query, key, value, query_t, key_t, value_t, weight, mask, probe,
    out_main, out_tan, out_trace,
    shards, queries, peak, acc_v, acc_t, sums, att, att_in, w_buf, probe_buf, part,
    z_out, z_in, x_out, x_in,
    swap_send, swap_recv, local_sem, load_sem, ring_send, ring_recv, share_send, share_recv,
    att_send, att_recv, w_send, w_recv, z_send, z_recv, x_send, x_recv,
):
    ctx = lax.axis_index("ctx")
    head = lax.axis_index("head")
    core, chip = ctx % 2, ctx // 2
    y, half = chip % RING, chip // RING
    z, xlo = head % RING, head // RING
    far = 1 - half
    width = weight.shape[1]
    wide = width // 2
    cols = wide // FLOWS

    sibling = {"ctx": chip * 2 + 1 - core, "head": head}
    opposite = {"ctx": (far * RING + y) * 2 + core, "head": head}
    y_next = [
        {"ctx": (half * RING + (y + step) % RING) * 2 + core, "head": head}
        for step in (1, RING - 1)
    ]
    z_next = [{"ctx": ctx, "head": xlo * RING + (z + step) % RING} for step in (1, RING - 1)]
    x_next = {"ctx": ctx, "head": (1 - xlo) * RING + z}
    fourth = {"ctx": (far * RING + y) * 2 + core, "head": (1 - xlo) * RING + z}

    mine = pl.ds(pl.multiple_of(half * HD, HD), HD)
    theirs = pl.ds(pl.multiple_of(far * HD, HD), HD)
    left, right = pl.ds(0, HD), pl.ds(HD, HD)

    def places(which):
        at = which * RING + y
        rows = pl.ds(pl.multiple_of(which * BLOCK, BLOCK), BLOCK)
        return [
            (key, shards.at[at, core, 0, :, left]),
            (key_t, shards.at[at, core, 0, :, right]),
            (value, shards.at[at, core, 1, :, left]),
            (value_t, shards.at[at, core, 1, :, right]),
            (query_t, queries.at[rows, left]),
            (query, queries.at[rows, right]),
        ]

    local = [
        pltpu.make_async_copy(src.at[:, mine], dst, local_sem.at[i])
        for i, (src, dst) in enumerate(places(half))
    ]
    for copy in local:
        copy.start()

    barrier = pltpu.get_barrier_semaphore()
    partners = [sibling, opposite] + y_next + z_next + [x_next, fourth]
    for partner in partners:
        pl.semaphore_signal(barrier, inc=1, device_id=partner, device_id_type=pl.DeviceIdType.MESH)
    pl.semaphore_wait(barrier, len(partners))

    def remote(src, dst, send, recv, device):
        return pltpu.make_async_remote_copy(
            src_ref=src, dst_ref=dst, send_sem=send, recv_sem=recv,
            device_id=device, device_id_type=pl.DeviceIdType.MESH,
        )

    def place(h, hop):
        which = half if h == 0 else far
        return which * RING + (y + hop + RING) % RING

    def message(d, h, k, e, arriving=False):
        sign = 1 if d == 0 else -1
        slot = place(h, -sign * (k + 1) if arriving else -sign * k)
        ref = shards.at[slot, core, e]
        return remote(ref, ref, ring_send.at[d, h, k, e], ring_recv.at[d, h, k, e], y_next[d])

    def share(h, hop, arriving=False):
        ref = shards.at[place(h, hop), 1 - core if arriving else core]
        return remote(ref, ref, share_send.at[h, hop % RING], share_recv.at[h, hop % RING], sibling)

    crossing = [
        remote(src.at[:, theirs], dst, swap_send.at[i], swap_recv.at[i], opposite)
        for i, (src, dst) in enumerate(places(half))
    ]
    landing = [
        remote(src.at[:, theirs], dst, swap_send.at[i], swap_recv.at[i], opposite)
        for i, (src, dst) in enumerate(places(far))
    ]
    for copy in crossing[:4]:
        copy.start()
    for e in range(2):
        for copy in local[2 * e : 2 * e + 2]:
            copy.wait()
        for d in range(2):
            message(d, 0, 0, e).start()
    share(0, 0).start()

    my_cols = pl.ds(pl.multiple_of(xlo * wide, wide), wide)
    its_cols = pl.ds(pl.multiple_of((1 - xlo) * wide, wide), wide)
    loads = [
        pltpu.make_async_copy(weight.at[at, my_cols], w_buf.at[i], load_sem.at[i])
        for i, at in enumerate([mine, theirs])
    ] + [pltpu.make_async_copy(probe, probe_buf, load_sem.at[2])]
    for copy in loads:
        copy.start()
    turn = (core + half) % 2
    w_fetch = remote(
        weight.at[pl.ds(pl.multiple_of(core * HD, HD), HD), its_cols], w_buf.at[2 + turn],
        w_send.at[0], w_recv.at[0], x_next,
    )

    def w_share(arriving=False):
        ref = w_buf.at[2 + (1 - turn if arriving else turn)]
        return remote(ref, ref, w_send.at[1], w_recv.at[1], sibling)

    peak[...] = jnp.full(peak.shape, MASKED, jnp.float32)
    sums[...] = jnp.zeros(sums.shape, jnp.float32)
    acc_v[...] = jnp.zeros(acc_v.shape, jnp.float32)
    acc_t[...] = jnp.zeros(acc_t.shape, jnp.float32)
    for copy in local[4:]:
        copy.wait()

    def split(x):
        high = x.astype(jnp.bfloat16)
        return high, (x - high.astype(jnp.float32)).astype(jnp.bfloat16)

    def attend(slot, blocks=(0, 1)):
        keys = jnp.concatenate([shards[slot, 0, 0], shards[slot, 1, 0]], axis=0)
        values = jnp.concatenate([shards[slot, 0, 1], shards[slot, 1, 1]], axis=0)
        ones = jnp.ones((PAIR, HD), jnp.bfloat16)
        value_one = jnp.concatenate([values[:, :HD], ones], axis=1)
        for r in blocks:
            at = pl.ds(pl.multiple_of(r * BLOCK, BLOCK), BLOCK)
            scores = dot_t(queries[at, HD:], keys[:, :HD]) * SCALE2
            slopes = dot_t(queries[at, :], keys)
            bias = [
                jnp.where(mask[(r * RING + y) * 2 + core, slot * 2 + b] == 1, 0.0, MASKED).astype(jnp.float32)
                for b in range(2)
            ]
            scores = jnp.concatenate(
                [scores[:, :BLOCK] + bias[0], scores[:, BLOCK:] + bias[1]], axis=1
            )
            old = peak[at, :]
            new = jnp.maximum(old, jnp.max(scores, axis=1, keepdims=True))
            fade = jnp.exp2(old - new)
            weights = jnp.exp2(scores - jnp.concatenate([new, new], axis=1))
            w_high, w_low = split(weights)
            t_high, t_low = split(weights * slopes)
            fade2 = jnp.concatenate([fade, fade], axis=1)
            peak[at, :] = new
            sums[at, :] = sums[at, :] * fade + jnp.sum(weights, axis=1, keepdims=True)
            acc_v[at, :] = acc_v[at, :] * fade2 + (dot(w_high, values) + dot(w_low, values))
            acc_t[at, :] = acc_t[at, :] * fade2 + (dot(t_high, value_one) + dot(t_low, value_one))

    def ring(h, k, e):
        for d in range(2):
            message(d, h, k, e, True).wait_recv()
            if k < 2 or e == d:
                message(d, h, k + 1, e).start()
        if e == 1:
            share(h, -k - 1).start()
            share(h, k + 1).start()

    def last(h):
        for d in range(2):
            message(d, h, 3, d, True).wait_recv()
        share(h, 4).start()

    def cross(e):
        for copy in landing[2 * e : 2 * e + 2]:
            copy.wait_recv()
        for d in range(2):
            message(d, 1, 0, e).start()
        if e == 1:
            share(1, 0).start()
            w_fetch.start()

    def send_rows():
        for copy in crossing[4:]:
            copy.start()

    def rows_of_opposite():
        for copy in landing[4:]:
            copy.wait_recv()

    def share_weight():
        w_fetch.wait_recv()
        w_share().start()

    do = functools.partial
    steps = [
        ([do(ring, 0, 0, 0), send_rows, do(ring, 0, 0, 1), do(cross, 0), do(cross, 1), rows_of_opposite], (0, 0)),
        ([do(ring, 0, 1, 0)], (1, 0)),
        ([do(ring, 0, 1, 1)], (0, -1)),
        ([do(ring, 1, 0, 0)], (0, 1)),
        ([do(ring, 1, 0, 1)], (0, -2)),
        ([do(ring, 0, 2, 0)], (0, 2)),
        ([do(ring, 0, 2, 1)], (1, -1)),
        ([do(ring, 1, 1, 0)], (1, 1)),
        ([do(ring, 1, 1, 1)], (0, -3)),
        ([do(last, 0)], (0, 3)),
        ([share_weight], (1, -2)),
        ([do(ring, 1, 2, 0)], (1, 2)),
        ([do(ring, 1, 2, 1)], (0, 4)),
        ([], (1, -3)),
        ([], (1, 3)),
        ([do(last, 1)], (1, 4)),
    ]

    def step(n, carry):
        slot = 0
        for i, (actions, here) in enumerate(steps):
            if i == len(steps) - 1:
                break
            slot = slot + jnp.where(n == i, place(*here), 0)

            @pl.when(n == i)
            def _(actions=actions, here=here):
                for action in actions:
                    action()
                share(*here, True).wait_recv()

        attend(slot)
        return carry

    lax.fori_loop(0, len(steps) - 1, step, 0)

    hand_back = [
        remote(att.at[which], att_in.at[i], att_send.at[i], att_recv.at[i], device)
        for i, (which, device) in enumerate([(far, opposite), (half, x_next), (far, fourth)])
    ]

    def attended(b):
        at = pl.ds(pl.multiple_of(b * BLOCK, BLOCK), BLOCK)
        total = sums[at, :]
        main = acc_v[at, :HD] / total
        tangent = (acc_v[at, HD:] + acc_t[at, :HD] * SCALE) / total - (
            acc_t[at, HD:] * SCALE
        ) / total * main
        pieces = []
        for zz in range(RING):
            for xx in range(2):
                first = (xx * RING + zz) * 8
                pieces += [main[first : first + 8], tangent[first : first + 8]]
        att[b] = jnp.concatenate(pieces, axis=0).astype(jnp.bfloat16)

    actions, here = steps[-1]
    for action in actions:
        action()
    share(*here, True).wait_recv()
    attend(place(*here), (far,))
    attended(far)
    hand_back[0].start()
    hand_back[2].start()
    attend(place(*here), (half,))
    attended(half)
    hand_back[1].start()

    for h in range(2):
        for d in range(2):
            for k in range(3):
                for e in range(2):
                    message(d, h, k, e).wait_send()
            message(d, h, 3, d).wait_send()
        for hop in range(-3, 5):
            share(h, hop).wait_send()
    for copy in crossing:
        copy.wait_send()
    for copy in loads:
        copy.wait()
    w_fetch.wait_send()
    w_share().wait_send()
    w_share(True).wait_recv()

    def project(f, begin):
        at = slice(f * cols, (f + 1) * cols)
        rows_in = [att[half], att_in[1]] if begin else [att_in[0], att_in[2]]
        lhs = jnp.concatenate(rows_in, axis=1)
        heads = (0, 2) if begin else (1, 3)
        term = dot(lhs, jnp.concatenate([w_buf[i, :, at] for i in heads], axis=0))
        part[:, at] = term if begin else part[:, at] + term

    chunk = 32

    def z_message(d, f, s):
        rows = pl.ds(0, chunk if s < 3 else chunk + 16)
        return remote(
            z_out.at[d, f, s, rows], z_in.at[d, f, s, rows], z_send.at[d, f, s], z_recv.at[d, f, s],
            z_next[d],
        )

    def send_sum(d, f, s, has_input):
        sign = 1 if d == 0 else -1
        target = (z + sign * (4 - s) + RING) % RING
        if has_input:
            z_message(d, f, s - 1).wait_recv()
        summed = part[
            pl.ds(pl.multiple_of(target * chunk, chunk), chunk), f * cols : (f + 1) * cols
        ]
        if has_input:
            summed = summed + z_in[d, f, s - 1, :chunk, :].astype(jnp.float32)
        high, low = split(summed)
        z_out[d, f, s, :chunk, :] = high
        if s == 3:
            low = low.astype(jnp.float32)
            z_out[d, f, s, chunk:, :] = jnp.concatenate([low[8:16], low[24:]], axis=0).astype(
                jnp.bfloat16
            )
        z_message(d, f, s).start()

    def far_side(f):
        return 1 if f < FLOWS // 2 else 0

    order = [f + side for f in range(FLOWS // 2) for side in (0, FLOWS // 2)]
    hand_back[1].wait()
    for f in order:
        project(f, True)
    hand_back[0].wait()
    hand_back[2].wait()
    for f in order:
        project(f, False)
        send_sum(far_side(f), f, 0, False)
        send_sum(1 - far_side(f), f, 1, False)
    for s in (1, 2, 3):
        for f in order:
            send_sum(far_side(f), f, s, True)
            if s < 3:
                send_sum(1 - far_side(f), f, s + 1, True)

    def x_message(f):
        return remote(x_out.at[f], x_in.at[f], x_send.at[f], x_recv.at[f], x_next)

    def settle(f, which):
        own = pl.ds(pl.multiple_of(which * 16, 16), 16)
        at = slice(f * cols, (f + 1) * cols)
        low = z_in[0, f, 3, chunk:, :].astype(jnp.float32) + z_in[1, f, 3, chunk:, :].astype(jnp.float32)
        low = jnp.where(which == 0, low[:8], low[8:])
        return (
            part[pl.ds(pl.multiple_of(z * chunk + which * 16, 16), 16), at]
            + z_in[0, f, 3, own, :].astype(jnp.float32)
            + z_in[1, f, 3, own, :].astype(jnp.float32)
            + jnp.concatenate([jnp.zeros_like(low), low], axis=0)
        )

    for f in order:
        for d in range(2):
            z_message(d, f, 3).wait_recv()
        high, low = split(settle(f, 1 - xlo))
        low = low.astype(jnp.float32)[8:]
        x_out[f, :16, :] = high
        x_out[f, 16:, :] = jnp.concatenate([low, jnp.zeros_like(low)], axis=0).astype(jnp.bfloat16)
        x_message(f).start()

    def finish(main, tangent, side, f, trace):
        at = pl.ds(pl.multiple_of(side * wide + f * cols, cols), cols)
        out_main[:, at] = main.astype(jnp.bfloat16)
        out_tan[:, at] = tangent.astype(jnp.bfloat16)
        signed = (2 * probe_buf[:, at] - 1).astype(jnp.float32) * tangent
        for i in range(cols // HD):
            trace = trace + signed[:, i * HD : (i + 1) * HD]
        return trace

    trace = jnp.zeros((8, HD), jnp.float32)
    for f in order:
        final = settle(f, xlo)
        trace = finish(final[:8], final[8:], xlo, f, trace)
    for f in order:
        x_message(f).wait_recv()
        final = x_in[f].astype(jnp.float32)
        trace = finish(final[:8], final[8:16] + final[16:24], 1 - xlo, f, trace)
    at_row = lax.broadcasted_iota(jnp.int32, (8, HD), 0) == lax.broadcasted_iota(jnp.int32, (8, HD), 1)
    sums_of = jnp.broadcast_to(jnp.sum(trace, axis=1, keepdims=True) / math.sqrt(width), (8, HD))
    out_trace[...] = jnp.sum(jnp.where(at_row, sums_of, 0.0), axis=0, keepdims=True)[:, :8]

    for d in range(2):
        for f in range(FLOWS):
            for s in range(0 if d == far_side(f) else 1, 4):
                z_message(d, f, s).wait_send()
    for f in range(FLOWS):
        x_message(f).wait_send()


def on_device(
    query, key, value, query_tangent, key_tangent, value_tangent, out_weight, block_mask, probe
):
    width = out_weight.shape[1]
    wide = width // 2
    cols = wide // FLOWS
    anywhere = pl.BlockSpec(memory_space=pl.ANY)
    in_vmem = pl.BlockSpec(memory_space=pltpu.VMEM)
    bf16, f32 = jnp.bfloat16, jnp.float32
    dma = pltpu.SemaphoreType.DMA
    main, tangent, trace = pl.pallas_call(
        kernel,
        out_shape=(
            jax.ShapeDtypeStruct((8, width), bf16),
            jax.ShapeDtypeStruct((8, width), bf16),
            jax.ShapeDtypeStruct((1, 8), f32),
        ),
        in_specs=[anywhere] * 7 + [pl.BlockSpec(memory_space=pltpu.SMEM), anywhere],
        out_specs=(in_vmem, in_vmem, in_vmem),
        scratch_shapes=[
            pltpu.VMEM((2 * RING, 2, 2, BLOCK, PAIR), bf16),
            pltpu.VMEM((PAIR, PAIR), bf16),
            pltpu.VMEM((PAIR, HD), f32),
            pltpu.VMEM((PAIR, PAIR), f32),
            pltpu.VMEM((PAIR, PAIR), f32),
            pltpu.VMEM((PAIR, HD), f32),
            pltpu.VMEM((2, PAIR, HD), bf16),
            pltpu.VMEM((3, PAIR, HD), bf16),
            pltpu.VMEM((4, HD, wide), bf16),
            pltpu.VMEM((8, width), jnp.int32),
            pltpu.VMEM((PAIR, wide), f32),
            pltpu.VMEM((2, FLOWS, 4, 48, cols), bf16),
            pltpu.VMEM((2, FLOWS, 4, 48, cols), bf16),
            pltpu.VMEM((FLOWS, 32, cols), bf16),
            pltpu.VMEM((FLOWS, 32, cols), bf16),
            dma((6,)), dma((6,)), dma((6,)), dma((3,)),
            dma((2, 2, 4, 2)), dma((2, 2, 4, 2)), dma((2, RING)), dma((2, RING)),
            dma((3,)), dma((3,)), dma((2,)), dma((2,)),
            dma((2, FLOWS, 4)), dma((2, FLOWS, 4)), dma((FLOWS,)), dma((FLOWS,)),
        ],
        compiler_params=pltpu.CompilerParams(
            collective_id=0, has_side_effects=True, vmem_limit_bytes=60 * 1024 * 1024
        ),
        cost_estimate=pl.CostEstimate(
            flops=3_000_000_000, bytes_accessed=4_000_000, transcendentals=1_100_000
        ),
    )(query, key, value, query_tangent, key_tangent, value_tangent, out_weight, block_mask, probe)

    def write(main_in, tangent_in, trace_in, main_out, tangent_out, trace_out):
        main_out[...] = main_in[...]
        tangent_out[...] = tangent_in[...]
        trace_out[...] = trace_in[...]

    main, tangent, trace = pl.pallas_call(
        write,
        out_shape=(
            jax.ShapeDtypeStruct((8, width), bf16),
            jax.ShapeDtypeStruct((8, width), bf16),
            jax.ShapeDtypeStruct((1, 8), f32),
        ),
        in_specs=[in_vmem] * 3,
        out_specs=[in_vmem] * 3,
    )(main, tangent, trace)
    return main, tangent, trace.reshape(8)


def solution(mesh):
    placed = (
        P("ctx", "head"),
        P("ctx", "head"),
        P("ctx", "head"),
        P("ctx", "head"),
        P("ctx", "head"),
        P("ctx", "head"),
        P("head", None),
        P(),
        P(("ctx", "head"), None),
    )
    return jax.shard_map(
        on_device,
        mesh=mesh,
        in_specs=placed,
        out_specs=(P(("ctx", "head"), None), P(("ctx", "head"), None), P(("ctx", "head"))),
        check_vma=False,
    )
```

```python
import functools
import math

import jax
import jax.numpy as jnp
from jax import lax
from jax.experimental import pallas as pl
from jax.experimental.pallas import tpu as pltpu
from jax.sharding import PartitionSpec as P

HD = 128
BLOCK = 128
RING = 8
PAIR = 2 * BLOCK
MASKED = -1e30
FLOWS = 4
SCALE = 1.0 / math.sqrt(HD)
SCALE2 = SCALE * math.log2(math.e)


def dot(a, b):
    return jnp.dot(a, b, preferred_element_type=jnp.float32)


def dot_t(a, b):
    return lax.dot_general(a, b, (((1,), (1,)), ((), ())), preferred_element_type=jnp.float32)


def kernel(
    query, key, value, query_t, key_t, value_t, weight, mask, probe,
    out_main, out_tan, out_trace,
    shards, queries, peak, acc_v, acc_t, sums, att, att_in, w_buf, probe_buf, part,
    z_out, z_in,
    swap_send, swap_recv, local_sem, load_sem, ring_send, ring_recv, share_send, share_recv,
    att_send, att_recv, w_send, w_recv, z_send, z_recv,
):
    ctx = lax.axis_index("ctx")
    head = lax.axis_index("head")
    core, chip = ctx % 2, ctx // 2
    y, half = chip % RING, chip // RING
    z, xlo = head % RING, head // RING
    far = 1 - half
    width = weight.shape[1]
    cols = width // FLOWS

    sibling = {"ctx": chip * 2 + 1 - core, "head": head}
    opposite = {"ctx": (far * RING + y) * 2 + core, "head": head}
    y_next = [
        {"ctx": (half * RING + (y + step) % RING) * 2 + core, "head": head}
        for step in (1, RING - 1)
    ]
    z_next = [{"ctx": ctx, "head": xlo * RING + (z + step) % RING} for step in (1, RING - 1)]
    x_next = {"ctx": ctx, "head": (1 - xlo) * RING + z}
    fourth = {"ctx": (far * RING + y) * 2 + core, "head": (1 - xlo) * RING + z}

    mine = pl.ds(pl.multiple_of(half * HD, HD), HD)
    theirs = pl.ds(pl.multiple_of(far * HD, HD), HD)
    left, right = pl.ds(0, HD), pl.ds(HD, HD)

    def places(which):
        at = which * RING + y
        rows = pl.ds(pl.multiple_of(which * BLOCK, BLOCK), BLOCK)
        return [
            (key, shards.at[at, core, 0, :, left]),
            (key_t, shards.at[at, core, 0, :, right]),
            (value, shards.at[at, core, 1, :, left]),
            (value_t, shards.at[at, core, 1, :, right]),
            (query_t, queries.at[rows, left]),
            (query, queries.at[rows, right]),
        ]

    local = [
        pltpu.make_async_copy(src.at[:, mine], dst, local_sem.at[i])
        for i, (src, dst) in enumerate(places(half))
    ]
    for copy in local:
        copy.start()

    barrier = pltpu.get_barrier_semaphore()
    partners = [sibling, opposite] + y_next + z_next + [x_next, fourth]
    for partner in partners:
        pl.semaphore_signal(barrier, inc=1, device_id=partner, device_id_type=pl.DeviceIdType.MESH)
    pl.semaphore_wait(barrier, len(partners))

    def remote(src, dst, send, recv, device):
        return pltpu.make_async_remote_copy(
            src_ref=src, dst_ref=dst, send_sem=send, recv_sem=recv,
            device_id=device, device_id_type=pl.DeviceIdType.MESH,
        )

    def place(h, hop):
        which = half if h == 0 else far
        return which * RING + (y + hop + RING) % RING

    def message(d, h, k, e, arriving=False):
        sign = 1 if d == 0 else -1
        slot = place(h, -sign * (k + 1) if arriving else -sign * k)
        ref = shards.at[slot, core, e]
        return remote(ref, ref, ring_send.at[d, h, k, e], ring_recv.at[d, h, k, e], y_next[d])

    def share(h, hop, arriving=False):
        ref = shards.at[place(h, hop), 1 - core if arriving else core]
        return remote(ref, ref, share_send.at[h, hop % RING], share_recv.at[h, hop % RING], sibling)

    crossing = [
        remote(src.at[:, theirs], dst, swap_send.at[i], swap_recv.at[i], opposite)
        for i, (src, dst) in enumerate(places(half))
    ]
    landing = [
        remote(src.at[:, theirs], dst, swap_send.at[i], swap_recv.at[i], opposite)
        for i, (src, dst) in enumerate(places(far))
    ]
    for copy in crossing[:4]:
        copy.start()
    for e in range(2):
        for copy in local[2 * e : 2 * e + 2]:
            copy.wait()
        for d in range(2):
            message(d, 0, 0, e).start()
    share(0, 0).start()

    loads = [
        pltpu.make_async_copy(weight.at[at], w_buf.at[i], load_sem.at[i])
        for i, at in enumerate([mine, theirs])
    ] + [pltpu.make_async_copy(probe, probe_buf, load_sem.at[2])]
    for copy in loads:
        copy.start()
    turn = (core + half) % 2
    w_rows = pl.ds(pl.multiple_of(core * HD, HD), HD)
    halves = [pl.ds(0, width // 2), pl.ds(width // 2, width // 2)]
    w_fetch = [
        remote(
            weight.at[w_rows, halves[i]], w_buf.at[2 + slot, :, halves[i]],
            w_send.at[i], w_recv.at[i], device,
        )
        for i, (slot, device) in enumerate([(turn, x_next), (1 - turn, fourth)])
    ]
    w_landing = [
        remote(
            weight.at[w_rows, halves[i]], w_buf.at[2 + turn, :, halves[i]],
            w_send.at[i], w_recv.at[i], device,
        )
        for i, device in enumerate([x_next, fourth])
    ]

    def w_share(arriving=False):
        ref = w_buf.at[2 + (1 - turn if arriving else turn)]
        return remote(ref, ref, w_send.at[2], w_recv.at[2], sibling)

    peak[...] = jnp.full(peak.shape, MASKED, jnp.float32)
    sums[...] = jnp.zeros(sums.shape, jnp.float32)
    acc_v[...] = jnp.zeros(acc_v.shape, jnp.float32)
    acc_t[...] = jnp.zeros(acc_t.shape, jnp.float32)
    for copy in local[4:]:
        copy.wait()

    def split(x):
        high = x.astype(jnp.bfloat16)
        return high, (x - high.astype(jnp.float32)).astype(jnp.bfloat16)

    def attend(slot, blocks=(0, 1)):
        keys = jnp.concatenate([shards[slot, 0, 0], shards[slot, 1, 0]], axis=0)
        values = jnp.concatenate([shards[slot, 0, 1], shards[slot, 1, 1]], axis=0)
        ones = jnp.ones((PAIR, HD), jnp.bfloat16)
        value_one = jnp.concatenate([values[:, :HD], ones], axis=1)
        for r in blocks:
            at = pl.ds(pl.multiple_of(r * BLOCK, BLOCK), BLOCK)
            scores = dot_t(queries[at, HD:], keys[:, :HD]) * SCALE2
            slopes = dot_t(queries[at, :], keys)
            bias = [
                jnp.where(mask[(r * RING + y) * 2 + core, slot * 2 + b] == 1, 0.0, MASKED).astype(jnp.float32)
                for b in range(2)
            ]
            scores = jnp.concatenate(
                [scores[:, :BLOCK] + bias[0], scores[:, BLOCK:] + bias[1]], axis=1
            )
            old = peak[at, :]
            new = jnp.maximum(old, jnp.max(scores, axis=1, keepdims=True))
            fade = jnp.exp2(old - new)
            weights = jnp.exp2(scores - jnp.concatenate([new, new], axis=1))
            w_high, w_low = split(weights)
            t_high, t_low = split(weights * slopes)
            fade2 = jnp.concatenate([fade, fade], axis=1)
            peak[at, :] = new
            sums[at, :] = sums[at, :] * fade + jnp.sum(weights, axis=1, keepdims=True)
            acc_v[at, :] = acc_v[at, :] * fade2 + (dot(w_high, values) + dot(w_low, values))
            acc_t[at, :] = acc_t[at, :] * fade2 + (dot(t_high, value_one) + dot(t_low, value_one))

    def ring(h, k, e):
        for d in range(2):
            message(d, h, k, e, True).wait_recv()
            if k < 2 or e == d:
                message(d, h, k + 1, e).start()
        if e == 1:
            share(h, -k - 1).start()
            share(h, k + 1).start()

    def last(h):
        for d in range(2):
            message(d, h, 3, d, True).wait_recv()
        share(h, 4).start()

    def cross(e):
        for copy in landing[2 * e : 2 * e + 2]:
            copy.wait_recv()
        for d in range(2):
            message(d, 1, 0, e).start()
        if e == 1:
            share(1, 0).start()
            for copy in w_fetch:
                copy.start()

    def send_rows():
        for copy in crossing[4:]:
            copy.start()

    def rows_of_opposite():
        for copy in landing[4:]:
            copy.wait_recv()

    def share_weight():
        for copy in w_landing:
            copy.wait_recv()
        w_share().start()

    do = functools.partial
    steps = [
        ([do(ring, 0, 0, 0), send_rows, do(ring, 0, 0, 1), do(cross, 0), do(cross, 1), rows_of_opposite], (0, 0)),
        ([do(ring, 0, 1, 0)], (1, 0)),
        ([do(ring, 0, 1, 1)], (0, -1)),
        ([do(ring, 1, 0, 0)], (0, 1)),
        ([do(ring, 1, 0, 1)], (0, -2)),
        ([do(ring, 0, 2, 0)], (0, 2)),
        ([do(ring, 0, 2, 1)], (1, -1)),
        ([do(ring, 1, 1, 0)], (1, 1)),
        ([do(ring, 1, 1, 1)], (0, -3)),
        ([do(last, 0)], (0, 3)),
        ([], (1, -2)),
        ([do(ring, 1, 2, 0)], (1, 2)),
        ([do(ring, 1, 2, 1)], (0, 4)),
        ([share_weight], (1, -3)),
        ([], (1, 3)),
        ([do(last, 1)], (1, 4)),
    ]

    def step(n, carry):
        slot = 0
        for i, (actions, here) in enumerate(steps):
            if i == len(steps) - 1:
                break
            slot = slot + jnp.where(n == i, place(*here), 0)

            @pl.when(n == i)
            def _(actions=actions, here=here):
                for action in actions:
                    action()
                share(*here, True).wait_recv()

        attend(slot)
        return carry

    lax.fori_loop(0, len(steps) - 1, step, 0)

    own_rows = pl.ds(pl.multiple_of(xlo * BLOCK, BLOCK), BLOCK)
    its_rows = pl.ds(pl.multiple_of((1 - xlo) * BLOCK, BLOCK), BLOCK)
    hand_back = [
        remote(att.at[which, rows], att_in.at[i], att_send.at[i], att_recv.at[i], device)
        for i, (which, rows, device) in enumerate(
            [(far, own_rows, opposite), (half, its_rows, x_next), (far, its_rows, fourth)]
        )
    ]

    def attended(b):
        at = pl.ds(pl.multiple_of(b * BLOCK, BLOCK), BLOCK)
        total = sums[at, :]
        main = acc_v[at, :HD] / total
        tangent = (acc_v[at, HD:] + acc_t[at, :HD] * SCALE) / total - (
            acc_t[at, HD:] * SCALE
        ) / total * main
        pieces = []
        for xx in range(2):
            for zz in range(RING):
                first = (xx * RING + zz) * 8
                pieces += [main[first : first + 8], tangent[first : first + 8]]
        att[b] = jnp.concatenate(pieces, axis=0).astype(jnp.bfloat16)

    actions, here = steps[-1]
    for action in actions:
        action()
    share(*here, True).wait_recv()
    attend(place(*here), (far,))
    attended(far)
    hand_back[0].start()
    hand_back[2].start()
    attend(place(*here), (half,))
    attended(half)
    hand_back[1].start()

    for h in range(2):
        for d in range(2):
            for k in range(3):
                for e in range(2):
                    message(d, h, k, e).wait_send()
            message(d, h, 3, d).wait_send()
        for hop in range(-3, 5):
            share(h, hop).wait_send()
    for copy in crossing:
        copy.wait_send()
    for copy in loads:
        copy.wait()
    for copy in w_fetch:
        copy.wait_send()
    w_share().wait_send()
    w_share(True).wait_recv()

    def project(f, begin):
        at = slice(f * cols, (f + 1) * cols)
        rows_in = [att[half, own_rows, :], att_in[2]] if begin else [att_in[0], att_in[1]]
        lhs = jnp.concatenate(rows_in, axis=1)
        heads = (0, 3) if begin else (1, 2)
        term = dot(lhs, jnp.concatenate([w_buf[i, :, at] for i in heads], axis=0))
        part[:, at] = term if begin else part[:, at] + term

    chunk = 16

    def z_message(d, f, s):
        rows = pl.ds(0, chunk if s < 3 else chunk + 16)
        return remote(
            z_out.at[d, f, s, rows], z_in.at[d, f, s, rows], z_send.at[d, f, s], z_recv.at[d, f, s],
            z_next[d],
        )

    def send_sum(d, f, s, has_input):
        sign = 1 if d == 0 else -1
        target = (z + sign * (4 - s) + RING) % RING
        if has_input:
            z_message(d, f, s - 1).wait_recv()
        summed = part[
            pl.ds(pl.multiple_of(target * chunk, chunk), chunk), f * cols : (f + 1) * cols
        ]
        if has_input:
            summed = summed + z_in[d, f, s - 1, :chunk, :].astype(jnp.float32)
        high, low = split(summed)
        z_out[d, f, s, :chunk, :] = high
        if s == 3:
            low = low.astype(jnp.float32)
            z_out[d, f, s, chunk:, :] = jnp.concatenate([low[8:], low[8:]], axis=0).astype(
                jnp.bfloat16
            )
        z_message(d, f, s).start()

    def far_side(f):
        return 1 if f < FLOWS // 2 else 0

    order = [f + side for f in range(FLOWS // 2) for side in (0, FLOWS // 2)]
    hand_back[2].wait()
    for f in order:
        project(f, True)
    hand_back[0].wait()
    hand_back[1].wait()
    for f in order:
        project(f, False)
        send_sum(far_side(f), f, 0, False)
        send_sum(1 - far_side(f), f, 1, False)
    for s in (1, 2, 3):
        for f in order:
            send_sum(far_side(f), f, s, True)
            if s < 3:
                send_sum(1 - far_side(f), f, s + 1, True)

    trace = jnp.zeros((8, HD), jnp.float32)
    for f in order:
        final = part[pl.ds(pl.multiple_of(z * chunk, chunk), chunk), f * cols : (f + 1) * cols]
        low = jnp.zeros((8, cols), jnp.float32)
        for d in range(2):
            z_message(d, f, 3).wait_recv()
            landed = z_in[d, f, 3].astype(jnp.float32)
            final = final + landed[:chunk]
            low = low + landed[chunk : chunk + 8]
        tangent = final[8:] + low
        at = slice(f * cols, (f + 1) * cols)
        out_main[:, at] = final[:8].astype(jnp.bfloat16)
        out_tan[:, at] = tangent.astype(jnp.bfloat16)
        signed = (2 * probe_buf[:, at] - 1).astype(jnp.float32) * tangent
        for i in range(cols // HD):
            trace = trace + signed[:, i * HD : (i + 1) * HD]
    at_row = lax.broadcasted_iota(jnp.int32, (8, HD), 0) == lax.broadcasted_iota(jnp.int32, (8, HD), 1)
    sums_of = jnp.broadcast_to(jnp.sum(trace, axis=1, keepdims=True) / math.sqrt(width), (8, HD))
    out_trace[...] = jnp.sum(jnp.where(at_row, sums_of, 0.0), axis=0, keepdims=True)[:, :8]

    for d in range(2):
        for f in range(FLOWS):
            for s in range(0 if d == far_side(f) else 1, 4):
                z_message(d, f, s).wait_send()


def on_device(
    query, key, value, query_tangent, key_tangent, value_tangent, out_weight, block_mask, probe
):
    width = out_weight.shape[1]
    cols = width // FLOWS
    anywhere = pl.BlockSpec(memory_space=pl.ANY)
    in_vmem = pl.BlockSpec(memory_space=pltpu.VMEM)
    bf16, f32 = jnp.bfloat16, jnp.float32
    dma = pltpu.SemaphoreType.DMA
    main, tangent, trace = pl.pallas_call(
        kernel,
        out_shape=(
            jax.ShapeDtypeStruct((8, width), bf16),
            jax.ShapeDtypeStruct((8, width), bf16),
            jax.ShapeDtypeStruct((1, 8), f32),
        ),
        in_specs=[anywhere] * 7 + [pl.BlockSpec(memory_space=pltpu.SMEM), anywhere],
        out_specs=(in_vmem, in_vmem, in_vmem),
        scratch_shapes=[
            pltpu.VMEM((2 * RING, 2, 2, BLOCK, PAIR), bf16),
            pltpu.VMEM((PAIR, PAIR), bf16),
            pltpu.VMEM((PAIR, HD), f32),
            pltpu.VMEM((PAIR, PAIR), f32),
            pltpu.VMEM((PAIR, PAIR), f32),
            pltpu.VMEM((PAIR, HD), f32),
            pltpu.VMEM((2, PAIR, HD), bf16),
            pltpu.VMEM((3, BLOCK, HD), bf16),
            pltpu.VMEM((4, HD, width), bf16),
            pltpu.VMEM((8, width), jnp.int32),
            pltpu.VMEM((BLOCK, width), f32),
            pltpu.VMEM((2, FLOWS, 4, 32, cols), bf16),
            pltpu.VMEM((2, FLOWS, 4, 32, cols), bf16),
            dma((6,)), dma((6,)), dma((6,)), dma((3,)),
            dma((2, 2, 4, 2)), dma((2, 2, 4, 2)), dma((2, RING)), dma((2, RING)),
            dma((3,)), dma((3,)), dma((3,)), dma((3,)),
            dma((2, FLOWS, 4)), dma((2, FLOWS, 4)),
        ],
        compiler_params=pltpu.CompilerParams(
            collective_id=0, has_side_effects=True, vmem_limit_bytes=60 * 1024 * 1024
        ),
        cost_estimate=pl.CostEstimate(
            flops=3_000_000_000, bytes_accessed=4_000_000, transcendentals=1_100_000
        ),
    )(query, key, value, query_tangent, key_tangent, value_tangent, out_weight, block_mask, probe)

    def write(main_in, tangent_in, trace_in, main_out, tangent_out, trace_out):
        main_out[...] = main_in[...]
        tangent_out[...] = tangent_in[...]
        trace_out[...] = trace_in[...]

    main, tangent, trace = pl.pallas_call(
        write,
        out_shape=(
            jax.ShapeDtypeStruct((8, width), bf16),
            jax.ShapeDtypeStruct((8, width), bf16),
            jax.ShapeDtypeStruct((1, 8), f32),
        ),
        in_specs=[in_vmem] * 3,
        out_specs=[in_vmem] * 3,
    )(main, tangent, trace)
    return main, tangent, trace.reshape(8)


def solution(mesh):
    placed = (
        P("ctx", "head"),
        P("ctx", "head"),
        P("ctx", "head"),
        P("ctx", "head"),
        P("ctx", "head"),
        P("ctx", "head"),
        P("head", None),
        P(),
        P(("ctx", "head"), None),
    )
    return jax.shard_map(
        on_device,
        mesh=mesh,
        in_specs=placed,
        out_specs=(P(("ctx", "head"), None), P(("ctx", "head"), None), P(("ctx", "head"))),
        check_vma=False,
    )
```

```python
import functools
import math

import jax
import jax.numpy as jnp
from jax import lax
from jax.experimental import pallas as pl
from jax.experimental.pallas import tpu as pltpu
from jax.sharding import PartitionSpec as P

HD = 128
BLOCK = 128
RING = 8
PAIR = 2 * BLOCK
MASKED = -1e30
FLOWS = 4
SCALE = 1.0 / math.sqrt(HD)
SCALE2 = SCALE * math.log2(math.e)


def dot(a, b):
    return jnp.dot(a, b, preferred_element_type=jnp.float32)


def dot_t(a, b):
    return lax.dot_general(a, b, (((1,), (1,)), ((), ())), preferred_element_type=jnp.float32)


def kernel(
    query, key, value, query_t, key_t, value_t, weight, mask, probe,
    out_main, out_tan, out_trace,
    shards, queries, peak, acc_v, acc_t, sums, att, att_in, w_buf, probe_buf, part,
    z_out, z_in,
    swap_send, swap_recv, local_sem, load_sem, ring_send, ring_recv, share_send, share_recv,
    att_send, att_recv, w_send, w_recv, z_send, z_recv,
):
    ctx = lax.axis_index("ctx")
    head = lax.axis_index("head")
    core, chip = ctx % 2, ctx // 2
    y, half = chip % RING, chip // RING
    z, xlo = head % RING, head // RING
    far = 1 - half
    width = weight.shape[1]
    cols = width // FLOWS

    sibling = {"ctx": chip * 2 + 1 - core, "head": head}
    opposite = {"ctx": (far * RING + y) * 2 + core, "head": head}
    y_next = [
        {"ctx": (half * RING + (y + step) % RING) * 2 + core, "head": head}
        for step in (1, RING - 1)
    ]
    z_next = [{"ctx": ctx, "head": xlo * RING + (z + step) % RING} for step in (1, RING - 1)]
    x_next = {"ctx": ctx, "head": (1 - xlo) * RING + z}
    fourth = {"ctx": (far * RING + y) * 2 + core, "head": (1 - xlo) * RING + z}

    mine = pl.ds(pl.multiple_of(half * HD, HD), HD)
    theirs = pl.ds(pl.multiple_of(far * HD, HD), HD)
    left, right = pl.ds(0, HD), pl.ds(HD, HD)

    def places(which):
        at = which * RING + y
        rows = pl.ds(pl.multiple_of(which * BLOCK, BLOCK), BLOCK)
        return [
            (key, shards.at[at, core, 0, :, left]),
            (key_t, shards.at[at, core, 0, :, right]),
            (value, shards.at[at, core, 1, :, left]),
            (value_t, shards.at[at, core, 1, :, right]),
            (query_t, queries.at[rows, left]),
            (query, queries.at[rows, right]),
        ]

    local = [
        pltpu.make_async_copy(src.at[:, mine], dst, local_sem.at[i])
        for i, (src, dst) in enumerate(places(half))
    ]
    for copy in local:
        copy.start()

    barrier = pltpu.get_barrier_semaphore()
    partners = [sibling, opposite] + y_next + z_next + [x_next, fourth]
    for partner in partners:
        pl.semaphore_signal(barrier, inc=1, device_id=partner, device_id_type=pl.DeviceIdType.MESH)
    pl.semaphore_wait(barrier, len(partners))

    def remote(src, dst, send, recv, device):
        return pltpu.make_async_remote_copy(
            src_ref=src, dst_ref=dst, send_sem=send, recv_sem=recv,
            device_id=device, device_id_type=pl.DeviceIdType.MESH,
        )

    def place(h, hop):
        which = half if h == 0 else far
        return which * RING + (y + hop + RING) % RING

    def message(d, h, k, e, arriving=False):
        sign = 1 if d == 0 else -1
        slot = place(h, -sign * (k + 1) if arriving else -sign * k)
        ref = shards.at[slot, core, e]
        return remote(ref, ref, ring_send.at[d, h, k, e], ring_recv.at[d, h, k, e], y_next[d])

    def share(h, hop, arriving=False):
        ref = shards.at[place(h, hop), 1 - core if arriving else core]
        return remote(ref, ref, share_send.at[h, hop % RING], share_recv.at[h, hop % RING], sibling)

    crossing = [
        remote(src.at[:, theirs], dst, swap_send.at[i], swap_recv.at[i], opposite)
        for i, (src, dst) in enumerate(places(half))
    ]
    landing = [
        remote(src.at[:, theirs], dst, swap_send.at[i], swap_recv.at[i], opposite)
        for i, (src, dst) in enumerate(places(far))
    ]
    for copy in crossing[:4]:
        copy.start()
    for e in range(2):
        for copy in local[2 * e : 2 * e + 2]:
            copy.wait()
        for d in range(2):
            message(d, 0, 0, e).start()
    share(0, 0).start()

    loads = [
        pltpu.make_async_copy(weight.at[at], w_buf.at[i], load_sem.at[i])
        for i, at in enumerate([mine, theirs])
    ] + [pltpu.make_async_copy(probe, probe_buf, load_sem.at[2])]
    for copy in loads:
        copy.start()
    turn = (core + half) % 2
    w_rows = pl.ds(pl.multiple_of(core * HD, HD), HD)
    halves = [pl.ds(0, width // 2), pl.ds(width // 2, width // 2)]
    w_fetch = [
        remote(
            weight.at[w_rows, halves[i]], w_buf.at[2 + slot, :, halves[i]],
            w_send.at[i], w_recv.at[i], device,
        )
        for i, (slot, device) in enumerate([(turn, x_next), (1 - turn, fourth)])
    ]
    w_landing = [
        remote(
            weight.at[w_rows, halves[i]], w_buf.at[2 + turn, :, halves[i]],
            w_send.at[i], w_recv.at[i], device,
        )
        for i, device in enumerate([x_next, fourth])
    ]

    def w_share(arriving=False):
        ref = w_buf.at[2 + (1 - turn if arriving else turn)]
        return remote(ref, ref, w_send.at[2], w_recv.at[2], sibling)

    peak[...] = jnp.full(peak.shape, MASKED, jnp.float32)
    sums[...] = jnp.zeros(sums.shape, jnp.float32)
    acc_v[...] = jnp.zeros(acc_v.shape, jnp.float32)
    acc_t[...] = jnp.zeros(acc_t.shape, jnp.float32)
    for copy in local[4:]:
        copy.wait()

    def split(x):
        high = x.astype(jnp.bfloat16)
        return high, (x - high.astype(jnp.float32)).astype(jnp.bfloat16)

    def attend(slot, blocks=(0, 1)):
        keys = jnp.concatenate([shards[slot, 0, 0], shards[slot, 1, 0]], axis=0)
        values = jnp.concatenate([shards[slot, 0, 1], shards[slot, 1, 1]], axis=0)
        ones = jnp.ones((PAIR, HD), jnp.bfloat16)
        value_one = jnp.concatenate([values[:, :HD], ones], axis=1)
        for r in blocks:
            at = pl.ds(pl.multiple_of(r * BLOCK, BLOCK), BLOCK)
            scores = dot_t(queries[at, HD:], keys[:, :HD]) * SCALE2
            slopes = dot_t(queries[at, :], keys)
            bias = [
                jnp.where(mask[(r * RING + y) * 2 + core, slot * 2 + b] == 1, 0.0, MASKED).astype(jnp.float32)
                for b in range(2)
            ]
            scores = jnp.concatenate(
                [scores[:, :BLOCK] + bias[0], scores[:, BLOCK:] + bias[1]], axis=1
            )
            old = peak[at, :]
            new = jnp.maximum(old, jnp.max(scores, axis=1, keepdims=True))
            fade = jnp.exp2(old - new)
            weights = jnp.exp2(scores - jnp.concatenate([new, new], axis=1))
            w_high, w_low = split(weights)
            t_high, t_low = split(weights * slopes)
            fade2 = jnp.concatenate([fade, fade], axis=1)
            peak[at, :] = new
            sums[at, :] = sums[at, :] * fade + jnp.sum(weights, axis=1, keepdims=True)
            acc_v[at, :] = acc_v[at, :] * fade2 + (dot(w_high, values) + dot(w_low, values))
            acc_t[at, :] = acc_t[at, :] * fade2 + (dot(t_high, value_one) + dot(t_low, value_one))

    def ring(h, k, e):
        for d in range(2):
            message(d, h, k, e, True).wait_recv()
            if k < 2 or e == d:
                message(d, h, k + 1, e).start()
        if e == 1:
            share(h, -k - 1).start()
            share(h, k + 1).start()

    def last(h):
        for d in range(2):
            message(d, h, 3, d, True).wait_recv()
        share(h, 4).start()

    def cross(e):
        for copy in landing[2 * e : 2 * e + 2]:
            copy.wait_recv()
        for d in range(2):
            message(d, 1, 0, e).start()
        if e == 1:
            share(1, 0).start()
            for copy in w_fetch:
                copy.start()

    def send_rows():
        for copy in crossing[4:]:
            copy.start()

    def rows_of_opposite():
        for copy in landing[4:]:
            copy.wait_recv()

    def share_weight():
        for copy in w_landing:
            copy.wait_recv()
        w_share().start()

    do = functools.partial
    steps = [
        (
            [do(ring, 0, 0, 0), send_rows, do(ring, 0, 0, 1), do(cross, 0), do(cross, 1)]
            + [do(ring, 0, 1, 0), rows_of_opposite],
            (0, 0),
        ),
        ([do(ring, 0, 1, 1)], (1, 0)),
        ([do(ring, 1, 0, 0)], (0, -1)),
        ([do(ring, 1, 0, 1)], (0, 1)),
        ([do(ring, 0, 2, 0)], (0, -2)),
        ([do(ring, 0, 2, 1)], (0, 2)),
        ([do(ring, 1, 1, 0)], (1, -1)),
        ([do(ring, 1, 1, 1)], (1, 1)),
        ([do(last, 0)], (0, -3)),
        ([], (0, 3)),
        ([do(ring, 1, 2, 0)], (1, -2)),
        ([do(ring, 1, 2, 1)], (1, 2)),
        ([], (0, 4)),
        ([share_weight], (1, -3)),
        ([], (1, 3)),
        ([do(last, 1)], (1, 4)),
    ]

    def step(n, carry):
        slot = 0
        for i, (actions, here) in enumerate(steps):
            if i == len(steps) - 1:
                break
            slot = slot + jnp.where(n == i, place(*here), 0)

            @pl.when(n == i)
            def _(actions=actions, here=here):
                for action in actions:
                    action()
                share(*here, True).wait_recv()

        attend(slot)
        return carry

    lax.fori_loop(0, len(steps) - 1, step, 0)

    own_rows = pl.ds(pl.multiple_of(xlo * BLOCK, BLOCK), BLOCK)
    its_rows = pl.ds(pl.multiple_of((1 - xlo) * BLOCK, BLOCK), BLOCK)
    hand_back = [
        remote(att.at[which, rows], att_in.at[i], att_send.at[i], att_recv.at[i], device)
        for i, (which, rows, device) in enumerate(
            [(far, own_rows, opposite), (half, its_rows, x_next), (far, its_rows, fourth)]
        )
    ]

    def attended(b):
        at = pl.ds(pl.multiple_of(b * BLOCK, BLOCK), BLOCK)
        total = sums[at, :]
        main = acc_v[at, :HD] / total
        tangent = (acc_v[at, HD:] + acc_t[at, :HD] * SCALE) / total - (
            acc_t[at, HD:] * SCALE
        ) / total * main
        pieces = []
        for xx in range(2):
            for zz in range(RING):
                first = (xx * RING + zz) * 8
                pieces += [main[first : first + 8], tangent[first : first + 8]]
        att[b] = jnp.concatenate(pieces, axis=0).astype(jnp.bfloat16)

    actions, here = steps[-1]
    for action in actions:
        action()
    share(*here, True).wait_recv()
    attend(place(*here), (far,))
    attended(far)
    hand_back[0].start()
    hand_back[2].start()
    attend(place(*here), (half,))
    attended(half)
    hand_back[1].start()

    for h in range(2):
        for d in range(2):
            for k in range(3):
                for e in range(2):
                    message(d, h, k, e).wait_send()
            message(d, h, 3, d).wait_send()
        for hop in range(-3, 5):
            share(h, hop).wait_send()
    for copy in crossing:
        copy.wait_send()
    for copy in loads:
        copy.wait()
    for copy in w_fetch:
        copy.wait_send()
    w_share().wait_send()
    w_share(True).wait_recv()

    def project(f, begin):
        at = slice(f * cols, (f + 1) * cols)
        rows_in = [att[half, own_rows, :], att_in[2]] if begin else [att_in[0], att_in[1]]
        lhs = jnp.concatenate(rows_in, axis=1)
        heads = (0, 3) if begin else (1, 2)
        term = dot(lhs, jnp.concatenate([w_buf[i, :, at] for i in heads], axis=0))
        part[:, at] = term if begin else part[:, at] + term

    chunk = 16

    def z_message(d, f, s):
        at = pl.ds(0, cols if s < 3 else cols + cols // 2)
        return remote(
            z_out.at[d, f, s, :, at], z_in.at[d, f, s, :, at], z_send.at[d, f, s],
            z_recv.at[d, f, s], z_next[d],
        )

    def send_sum(d, f, s, has_input):
        sign = 1 if d == 0 else -1
        target = (z + sign * (4 - s) + RING) % RING
        if has_input:
            z_message(d, f, s - 1).wait_recv()
        summed = part[
            pl.ds(pl.multiple_of(target * chunk, chunk), chunk), f * cols : (f + 1) * cols
        ]
        if has_input:
            summed = summed + z_in[d, f, s - 1, :, :cols].astype(jnp.float32)
        high, low = split(summed)
        z_out[d, f, s, :, :cols] = high
        if s == 3:
            low = low.astype(jnp.float32)[8:]
            z_out[d, f, s, :, cols:] = jnp.concatenate(
                [low[:, : cols // 2], low[:, cols // 2 :]], axis=0
            ).astype(jnp.bfloat16)
        z_message(d, f, s).start()

    def far_side(f):
        return 1 if f < FLOWS // 2 else 0

    order = [f + side for f in range(FLOWS // 2) for side in (0, FLOWS // 2)]
    hand_back[2].wait()
    for f in order:
        project(f, True)
    hand_back[0].wait()
    hand_back[1].wait()
    for f in order:
        project(f, False)
        send_sum(far_side(f), f, 0, False)
        send_sum(1 - far_side(f), f, 1, False)
    for s in (1, 2, 3):
        for f in order:
            send_sum(far_side(f), f, s, True)
            if s < 3:
                send_sum(1 - far_side(f), f, s + 1, True)

    trace = jnp.zeros((8, HD), jnp.float32)
    for f in order:
        final = part[pl.ds(pl.multiple_of(z * chunk, chunk), chunk), f * cols : (f + 1) * cols]
        low = jnp.zeros((8, cols), jnp.float32)
        for d in range(2):
            z_message(d, f, 3).wait_recv()
            landed = z_in[d, f, 3].astype(jnp.float32)
            final = final + landed[:, :cols]
            low = low + jnp.concatenate([landed[:8, cols:], landed[8:, cols:]], axis=1)
        tangent = final[8:] + low
        at = slice(f * cols, (f + 1) * cols)
        out_main[:, at] = final[:8].astype(jnp.bfloat16)
        out_tan[:, at] = tangent.astype(jnp.bfloat16)
        signed = (2 * probe_buf[:, at] - 1).astype(jnp.float32) * tangent
        for i in range(cols // HD):
            trace = trace + signed[:, i * HD : (i + 1) * HD]
    at_row = lax.broadcasted_iota(jnp.int32, (8, HD), 0) == lax.broadcasted_iota(jnp.int32, (8, HD), 1)
    sums_of = jnp.broadcast_to(jnp.sum(trace, axis=1, keepdims=True) / math.sqrt(width), (8, HD))
    out_trace[...] = jnp.sum(jnp.where(at_row, sums_of, 0.0), axis=0, keepdims=True)[:, :8]

    for d in range(2):
        for f in range(FLOWS):
            for s in range(0 if d == far_side(f) else 1, 4):
                z_message(d, f, s).wait_send()


def on_device(
    query, key, value, query_tangent, key_tangent, value_tangent, out_weight, block_mask, probe
):
    width = out_weight.shape[1]
    cols = width // FLOWS
    anywhere = pl.BlockSpec(memory_space=pl.ANY)
    in_vmem = pl.BlockSpec(memory_space=pltpu.VMEM)
    bf16, f32 = jnp.bfloat16, jnp.float32
    dma = pltpu.SemaphoreType.DMA
    main, tangent, trace = pl.pallas_call(
        kernel,
        out_shape=(
            jax.ShapeDtypeStruct((8, width), bf16),
            jax.ShapeDtypeStruct((8, width), bf16),
            jax.ShapeDtypeStruct((1, 8), f32),
        ),
        in_specs=[anywhere] * 7 + [pl.BlockSpec(memory_space=pltpu.SMEM), anywhere],
        out_specs=(in_vmem, in_vmem, in_vmem),
        scratch_shapes=[
            pltpu.VMEM((2 * RING, 2, 2, BLOCK, PAIR), bf16),
            pltpu.VMEM((PAIR, PAIR), bf16),
            pltpu.VMEM((PAIR, HD), f32),
            pltpu.VMEM((PAIR, PAIR), f32),
            pltpu.VMEM((PAIR, PAIR), f32),
            pltpu.VMEM((PAIR, HD), f32),
            pltpu.VMEM((2, PAIR, HD), bf16),
            pltpu.VMEM((3, BLOCK, HD), bf16),
            pltpu.VMEM((4, HD, width), bf16),
            pltpu.VMEM((8, width), jnp.int32),
            pltpu.VMEM((BLOCK, width), f32),
            pltpu.VMEM((2, FLOWS, 4, 16, cols + cols // 2), bf16),
            pltpu.VMEM((2, FLOWS, 4, 16, cols + cols // 2), bf16),
            dma((6,)), dma((6,)), dma((6,)), dma((3,)),
            dma((2, 2, 4, 2)), dma((2, 2, 4, 2)), dma((2, RING)), dma((2, RING)),
            dma((3,)), dma((3,)), dma((3,)), dma((3,)),
            dma((2, FLOWS, 4)), dma((2, FLOWS, 4)),
        ],
        compiler_params=pltpu.CompilerParams(
            collective_id=0, has_side_effects=True, vmem_limit_bytes=60 * 1024 * 1024
        ),
        cost_estimate=pl.CostEstimate(
            flops=3_000_000_000, bytes_accessed=4_000_000, transcendentals=1_100_000
        ),
    )(query, key, value, query_tangent, key_tangent, value_tangent, out_weight, block_mask, probe)

    def write(main_in, tangent_in, trace_in, main_out, tangent_out, trace_out):
        main_out[...] = main_in[...]
        tangent_out[...] = tangent_in[...]
        trace_out[...] = trace_in[...]

    main, tangent, trace = pl.pallas_call(
        write,
        out_shape=(
            jax.ShapeDtypeStruct((8, width), bf16),
            jax.ShapeDtypeStruct((8, width), bf16),
            jax.ShapeDtypeStruct((1, 8), f32),
        ),
        in_specs=[in_vmem] * 3,
        out_specs=[in_vmem] * 3,
    )(main, tangent, trace)
    return main, tangent, trace.reshape(8)


def solution(mesh):
    placed = (
        P("ctx", "head"),
        P("ctx", "head"),
        P("ctx", "head"),
        P("ctx", "head"),
        P("ctx", "head"),
        P("ctx", "head"),
        P("head", None),
        P(),
        P(("ctx", "head"), None),
    )
    return jax.shard_map(
        on_device,
        mesh=mesh,
        in_specs=placed,
        out_specs=(P(("ctx", "head"), None), P(("ctx", "head"), None), P(("ctx", "head"))),
        check_vma=False,
    )
```
